32 devices in a mesh: gx: 8 (over z, x), gy: 4 (over y, core).
Axes of the slice: x: 2, y: 2, z: 4, core: 2. Of those that a mesh axis runs over, the one named last changes fastest.
Arguments:
- spheres: float32 [13, 4, 64, 128], P(None, 'gy', 'gx')
- new_home: int32 [4, 64], P('gy', 'gx'), may hold values from 0 to 63, as said below
- ghost_list: int32 [4, 16], P('gy', 'gx'), may hold values from 0 to 7, as said below
- tile_pairs: int32 [4, 2048, 2], P('gy', 'gx'), may hold values from 0 to 25, as said below
- tile_count: int32 [4, 8], P('gy', 'gx'), may hold values from 24 to 256
Outputs:
- updated: float32 [13, 4, 64, 128], P(None, 'gy', 'gx')
The draws below stay inside these ranges and needn't reach their ends.
Inputs may be any that keep to these rules, and one draw needn't show every extreme that they name: Within each row new_home is a permutation of the row's slots; a block in slot b moves to the device 0 to 3 slabs ahead along gx, cyclically; some block moves exactly 3 slabs. `ghost_list`: the 2 entries of one device are distinct. `tile_pairs`: column 0 is a local block; column 1 is a pool entry below 16 or from 18 on; every such pool entry appears in a valid tile of every device.
All inputs are finite; a program needn't handle non-finite values.
Results may differ from the reference program's by a relative error of at most 0.0003.
Values sent between devices are 32-bit elements; how exact they have to be, the bound alone decides.
A program may use at most 64 MiB of HBM per device.

```python
import jax
import jax.numpy as jnp
from jax import lax

BLOCK = 128
DEVICE_BLOCKS = 8
GHOST = 2
TILE_CAP = 256
N_GX = 8
N_GY = 4


def draw_spheres(key, part):
    random_keys = jax.random.split(key, 5)
    shape_one = (N_GY, N_GX * DEVICE_BLOCKS, BLOCK)
    position = jax.random.uniform(random_keys[0], (3,) + shape_one, dtype=jnp.float32)
    velocity = jax.random.normal(random_keys[1], (3,) + shape_one)
    angular = 3.0 * jax.random.normal(random_keys[2], (3,) + shape_one)
    accel = 2.0 * jax.random.normal(random_keys[3], (3,) + shape_one)
    radius = jax.random.uniform(random_keys[4], (1,) + shape_one, minval=0.08, maxval=0.12)
    return jnp.concatenate([position, velocity, angular, accel, radius], 0).astype(jnp.float32)


def draw_new_home(key, part):
    slab_windows = N_GX // 2
    pair_len = 2 * DEVICE_BLOCKS
    random_keys = jax.random.split(key, N_GY * slab_windows + N_GY)

    def one_window(wkey):
        perm = jax.random.permutation(wkey, pair_len)
        final_position = jnp.argmax(perm == pair_len - 1)
        perm = perm.at[final_position].set(perm[0])
        return perm.at[0].set(pair_len - 1)
    perms = jax.vmap(one_window)(random_keys[:N_GY * slab_windows]).reshape(N_GY, slab_windows, pair_len)
    base = (jnp.arange(slab_windows, dtype=jnp.int32) * pair_len)[None, :, None]
    slab_offsets = jax.vmap(lambda sphere_key: jax.random.randint(sphere_key, (), 1, DEVICE_BLOCKS))(random_keys[N_GY * slab_windows:])
    home = (perms + base).reshape(N_GY, N_GX * DEVICE_BLOCKS) + (slab_offsets + DEVICE_BLOCKS)[:, None]
    return (home % (N_GX * DEVICE_BLOCKS)).astype(jnp.int32)


def draw_ghost_list(key, part):
    random_keys = jax.random.split(key, N_GY * N_GX)
    picks = jax.vmap(lambda gkey: jax.random.permutation(gkey, DEVICE_BLOCKS)[:GHOST])(random_keys)
    return picks.reshape(N_GY, N_GX * GHOST).astype(jnp.int32)


def draw_tile_pairs(key, part):
    valid_pool = DEVICE_BLOCKS + 8 * GHOST
    random_keys = jax.random.split(key, N_GY * N_GX)

    def one_device(dkey):
        first, second, third = jax.random.split(dkey, 3)
        left_idx = jax.random.randint(first, (TILE_CAP,), 0, DEVICE_BLOCKS)
        entry = jnp.concatenate([jax.random.permutation(second, valid_pool), jax.random.randint(third, (TILE_CAP - valid_pool,), 0, valid_pool)])
        right_idx = jnp.where(entry < DEVICE_BLOCKS + 4 * GHOST, entry, entry + GHOST)
        return jnp.stack([left_idx, right_idx], 1)
    pairs = jax.vmap(one_device)(random_keys)
    return pairs.reshape(N_GY, N_GX * TILE_CAP, 2).astype(jnp.int32)


def draw_tile_count(key, part):
    valid_pool = DEVICE_BLOCKS + 8 * GHOST
    random_keys = jax.random.split(key, 4)
    spread = TILE_CAP - valid_pool + 1
    first = jax.random.randint(random_keys[0], (N_GY * N_GX,), 0, spread)
    second = jax.random.randint(random_keys[1], (N_GY * N_GX,), 0, spread)
    third = jax.random.randint(random_keys[2], (N_GY * N_GX,), 0, spread)
    counts = valid_pool + jnp.minimum(jnp.minimum(first, second), third)
    chosen = jax.random.randint(random_keys[3], (), 0, N_GY * N_GX)
    counts = counts.at[chosen].set(TILE_CAP)
    counts = counts.at[(chosen + 1) % (N_GY * N_GX)].set(valid_pool)
    return counts.reshape(N_GY, N_GX).astype(jnp.int32)


def setup_inputs(seed: int = 0) -> dict:
    keys = jax.random.split(jax.random.key(seed), 6)
    spheres = draw_spheres(jax.random.fold_in(keys[5], 71), 0)
    new_home = draw_new_home(jax.random.fold_in(keys[5], 71), 0)
    ghost_list = draw_ghost_list(jax.random.fold_in(keys[5], 71), 0)
    tile_pairs = draw_tile_pairs(jax.random.fold_in(keys[5], 71), 0)
    tile_count = draw_tile_count(jax.random.fold_in(keys[5], 71), 0)
    return {"spheres": spheres, "new_home": new_home, "ghost_list": ghost_list, "tile_pairs": tile_pairs, "tile_count": tile_count}


time_step = 0.01
stiffness = 200.0
damp_normal = 20.0
damp_tangent = 10.0
cohesion = 10.0
density = 240.0

def cross_three(left, right):
    return jnp.stack([left[1] * right[2] - left[2] * right[1], left[2] * right[0] - left[0] * right[2], left[0] * right[1] - left[1] * right[0]], 0)

def contact(part_left, right_particle, same_block):
    width = part_left.shape[1]
    sep = part_left[0:3, :, None] - right_particle[0:3, None, :]
    dist = jnp.sqrt(lax.optimization_barrier(jnp.sum(sep * sep, 0)))
    rad_left = part_left[12][:, None]
    rad_right = right_particle[12][None, :]
    depth = rad_left + rad_right - dist
    diagonal = jnp.eye(width, dtype=bool)
    touch = (depth > 0) & jnp.logical_not(same_block & diagonal)
    safe_dist = jnp.where(touch, dist, 1.0)
    normal = jnp.where(touch[None], sep / safe_dist[None], 0.0)
    depth = jnp.where(touch, depth, 0.0)
    reduced = rad_left * rad_right / (rad_left + rad_right)
    contact_rad = jnp.sqrt(reduced * depth)
    spin = part_left[6:9, :, None] * rad_left[None] + right_particle[6:9, None, :] * rad_right[None]
    relative = part_left[3:6, :, None] - right_particle[3:6, None, :] - cross_three(spin, normal)
    normal_speed = lax.optimization_barrier(jnp.sum(relative * normal, 0))
    tangent = relative - normal_speed[None] * normal
    normal_force = stiffness * contact_rad * depth - damp_normal * contact_rad * normal_speed - cohesion * contact_rad
    tangent_force = -damp_tangent * contact_rad[None] * tangent
    force = lax.optimization_barrier(jnp.sum(normal_force[None] * normal + tangent_force, 2))
    torque = lax.optimization_barrier(jnp.sum(-rad_left[None] * cross_three(normal, tangent_force), 2))
    return jnp.concatenate([force, torque], 0)

def advance(drifted, forces_sum):
    radius = drifted[12:13]
    mass = density * (4.0 / 3.0) * jnp.pi * radius ** 3
    inertia = 0.4 * mass * radius * radius
    gravity_vec = jnp.array([0.0, 0.0, -1.0], dtype=drifted.dtype).reshape((3,) + (1,) * (drifted.ndim - 1))
    accel = forces_sum[0:3] / mass + gravity_vec
    velocity = drifted[3:6] + 0.5 * time_step * (drifted[9:12] + accel)
    angular = drifted[6:9] + time_step * forces_sum[3:6] / inertia
    return jnp.concatenate([drifted[0:3], velocity, angular, accel, radius], 0)

def reference(spheres, new_home, ghost_list, tile_pairs, tile_count):

    def move_row(row_data, row_home):
        return jnp.zeros_like(row_data).at[:, row_home].add(row_data)
    moved_blocks = jax.vmap(move_row, in_axes=(1, 0), out_axes=1)(spheres, new_home)
    position = moved_blocks[0:3] + time_step * moved_blocks[3:6] + 0.5 * time_step * time_step * moved_blocks[9:12]
    drifted = jnp.concatenate([position, moved_blocks[3:]], 0)
    grid = drifted.reshape(13, N_GY, N_GX, DEVICE_BLOCKS, BLOCK)
    picks = ghost_list.reshape(N_GY, N_GX, GHOST).astype(jnp.int32)
    picks = jnp.broadcast_to(picks[None, :, :, :, None], (13, N_GY, N_GX, GHOST, BLOCK))
    ghosts = jnp.take_along_axis(grid, picks, axis=3)
    shells = []
    for row_step in (-1, 0, 1):
        for col_step in (-1, 0, 1):
            shells.append(jnp.roll(ghosts, (-row_step, -col_step), axis=(1, 2)))
    shell_all = jnp.stack(shells, 3).reshape(13, N_GY, N_GX, 9 * GHOST, BLOCK)
    pool_all = jnp.concatenate([grid, shell_all], 3)
    pool_entries = DEVICE_BLOCKS + 9 * GHOST
    pool_dev = pool_all.transpose(1, 2, 0, 3, 4).reshape(N_GY * N_GX, 13, pool_entries, BLOCK)
    pairs_dev = tile_pairs.reshape(N_GY * N_GX, TILE_CAP, 2)
    counts_dev = tile_count.reshape(N_GY * N_GX)

    def one_device(inputs):
        pool_one, pairs_one, count_one = inputs

        def tile_step(index, forces_sum):
            left_idx = pairs_one[index, 0]
            right_idx = pairs_one[index, 1]
            terms = contact(pool_one[:, left_idx], pool_one[:, right_idx], left_idx == right_idx)
            return forces_sum.at[:, left_idx].add(terms)
        start = jnp.zeros((6, DEVICE_BLOCKS, BLOCK), dtype=pool_one.dtype)
        return lax.fori_loop(0, count_one, tile_step, start)
    totals = lax.map(one_device, (pool_dev, pairs_dev, counts_dev))
    totals = totals.reshape(N_GY, N_GX, 6, DEVICE_BLOCKS, BLOCK).transpose(2, 0, 1, 3, 4)
    totals = totals.reshape(6, N_GY, N_GX * DEVICE_BLOCKS, BLOCK)
    return advance(drifted, totals)
```

```python
import functools

import jax
import jax.numpy as jnp
from jax import lax
from jax.experimental import pallas as pl
from jax.experimental.pallas import tpu as pltpu
from jax.sharding import PartitionSpec as P

SPAN = 3
MESH = pl.DeviceIdType.MESH

time_step = 0.01
stiffness = 200.0
damp_normal = 20.0
damp_tangent = 10.0
cohesion = 10.0
density = 240.0

ROWS = 16
FEATURES = 11


def exchange_kernel(
    spheres, home, lent_list, pairs, count, drifted, pool, counts, sections, arrived, mine, lent, send_sem, recv_sem, gsend_sem, grecv_sem
):
    comps, blocks, width = spheres.shape
    ghosts = lent_list.shape[1]
    nx = lax.axis_size("gx")
    ny = lax.axis_size("gy")
    gx = lax.axis_index("gx")
    gy = lax.axis_index("gy")

    def peer(dx, dy):
        return {"gx": lax.rem(gx + dx + nx, nx), "gy": lax.rem(gy + dy + ny, ny)}

    steps = [(dr, dg) for dr in (-1, 0, 1) for dg in (-1, 0, 1)]
    barrier = pltpu.get_barrier_semaphore()
    for dr, dg in steps:
        if (dr, dg) != (0, 0):
            pl.semaphore_signal(barrier, inc=1, device_id=peer(dg, dr), device_id_type=MESH)
    for off in range(2, SPAN + 1):
        pl.semaphore_signal(barrier, inc=1, device_id=peer(-off, 0), device_id_type=MESH)

    slot = lax.broadcasted_iota(jnp.int32, (blocks, width), 0)
    for off in range(SPAN, -1, -1):
        want = slot + lax.rem(gx + off, nx) * blocks
        masks = [want == home[0, b] for b in range(blocks)]
        for c in range(comps):
            row = jnp.zeros((blocks, width), jnp.float32)
            for b in range(blocks):
                row = jnp.where(masks[b], jnp.broadcast_to(spheres[c, b : b + 1, :], (blocks, width)), row)
            sections[off, c] = row

    pl.semaphore_wait(barrier, 8 + SPAN - 1)
    copies = []
    for off in range(SPAN, 0, -1):
        copy = pltpu.make_async_remote_copy(
            src_ref=sections.at[off],
            dst_ref=arrived.at[off - 1],
            send_sem=send_sem.at[off - 1],
            recv_sem=recv_sem.at[off - 1],
            device_id=peer(off, 0),
            device_id_type=MESH,
        )
        copy.start()
        copies.append(copy)

    cap = pairs.shape[1]
    valid = lax.broadcasted_iota(jnp.int32, (1, cap), 1) < count[0, 0]
    left = jnp.where(valid, pairs[0:1, :], -1)
    right = jnp.where(valid, pairs[1:2, :], -1)
    hot_left = (lax.broadcasted_iota(jnp.int32, (blocks, cap), 0) == left).astype(jnp.float32)
    hot_right = (lax.broadcasted_iota(jnp.int32, (width, cap), 0) == right).astype(jnp.float32)
    counts[...] = lax.dot_general(
        hot_left, hot_right, (((1,), (1,)), ((), ())), preferred_element_type=jnp.float32
    ).astype(jnp.int32)

    for copy in copies:
        copy.wait()

    def moved(c):
        total = sections[0, c]
        for off in range(SPAN):
            total = total + arrived[off, c]
        return total

    rows = [moved(c) for c in range(comps)]
    for c in range(3):
        rows[c] = rows[c] + time_step * rows[3 + c] + 0.5 * time_step * time_step * rows[9 + c]
    for c in range(comps):
        drifted[c] = rows[c]
    scale = stiffness / cohesion
    radius = rows[12]
    feats = [scale * rows[c] for c in range(3)] + [rows[c] for c in range(3, 6)]
    feats += [radius * rows[c] for c in range(6, 9)] + [scale * radius, 1.0 / (scale * radius)]
    mine[...] = jnp.zeros_like(mine)
    for f in range(FEATURES):
        for b in range(blocks):
            mine[b, f : f + 1, :] = feats[f][b : b + 1, :]
    pool[0:blocks] = mine[...]
    for g in range(ghosts):
        lent[g] = mine[lent_list[0, g]]
        pool[blocks + 4 * ghosts + g] = jnp.zeros((ROWS, width), jnp.float32)
    copies = []
    for k, (dr, dg) in enumerate(steps):
        if (dr, dg) == (0, 0):
            continue
        copy = pltpu.make_async_remote_copy(
            src_ref=lent,
            dst_ref=pool.at[pl.ds(blocks + k * ghosts, ghosts)],
            send_sem=gsend_sem.at[k],
            recv_sem=grecv_sem.at[k],
            device_id=peer(-dg, -dr),
            device_id_type=MESH,
        )
        copy.start()
        copies.append(copy)
    for copy in copies:
        copy.wait()


def pair_sums(left, spread, chunk, same):
    xa, va, ua, ra, ia = left[0:3], left[3:6], left[6:9], left[9], left[10]
    rows = pl.ds(chunk * 8, 8)
    xb = [spread[c, rows, :] for c in range(0, 3)]
    vb = [spread[c, rows, :] for c in range(3, 6)]
    ub = [spread[c, rows, :] for c in range(6, 9)]
    rb, ib = spread[9, rows, :], spread[10, rows, :]
    sep = [xa[c] - xb[c] for c in range(3)]
    square = sep[0] * sep[0] + sep[1] * sep[1] + sep[2] * sep[2]
    inv = lax.rsqrt(square)
    depth = (ra + rb) - square * inv
    touch = depth > 0
    if same:
        shape = square.shape
        own = lax.broadcasted_iota(jnp.int32, shape, 0) + chunk * 8 == lax.broadcasted_iota(jnp.int32, shape, 1)
        touch = jnp.logical_and(touch, jnp.logical_not(own))
    rc = jnp.where(touch, depth * lax.rsqrt(depth * (ia + ib)), 0.0)
    inv = jnp.where(touch, inv, 0.0)
    depth = jnp.where(touch, depth, 0.0)
    n = [s * inv for s in sep]
    dv = [va[c] - vb[c] for c in range(3)]
    spin = [ua[c] + ub[c] for c in range(3)]
    vn = dv[0] * n[0] + dv[1] * n[1] + dv[2] * n[2]
    slip = [
        rc * (dv[0] - (spin[1] * n[2] - spin[2] * n[1])),
        rc * (dv[1] - (spin[2] * n[0] - spin[0] * n[2])),
        rc * (dv[2] - (spin[0] * n[1] - spin[1] * n[0])),
    ]
    push = rc * (depth - 1.0 - vn)
    return [push * n[c] - slip[c] for c in range(3)] + [
        n[1] * slip[2] - n[2] * slip[1],
        n[2] * slip[0] - n[0] * slip[2],
        n[0] * slip[1] - n[1] * slip[0],
    ]


def contact_kernel(ghosts, counts, drifted, pool, out, spread, acc, sums):
    comps, blocks, width = drifted.shape
    entries = pool.shape[0]
    acc[...] = jnp.zeros_like(acc)

    def tile(i, j, weight, same):
        left = [jnp.broadcast_to(pool[i, f : f + 1, :], (8, width)) for f in range(FEATURES)]
        total = [jnp.zeros((8, width), jnp.float32)] * 6
        for chunk in range(width // 8):
            part = pair_sums(left, spread, chunk, same)
            total = [total[c] + part[c] for c in range(6)]
        for c in range(6):
            acc[i, c] = acc[i, c] + weight * total[c]

    def entry_step(step, carry):
        j = jnp.where(step < blocks + 4 * ghosts, step, step + ghosts)
        columns = jnp.transpose(pool[j])
        for f in range(FEATURES):
            spread[f] = jnp.broadcast_to(columns[:, f : f + 1], (width, width))

        def block_step(i, inner):
            number = counts[i, j]
            weight = number.astype(jnp.float32)

            @pl.when(jnp.logical_and(number > 0, i != j))
            def _():
                tile(i, j, weight, False)

            @pl.when(jnp.logical_and(number > 0, i == j))
            def _():
                tile(i, j, weight, True)

            return inner

        return lax.fori_loop(0, blocks, block_step, carry)

    lax.fori_loop(0, entries - ghosts, entry_step, 0)

    for i in range(blocks):
        for c in range(6):
            sums[c, i : i + 1, :] = jnp.sum(acc[i, c], axis=0, keepdims=True)
    radius = drifted[12]
    mass = density * (4.0 / 3.0) * jnp.pi * radius * radius * radius
    inertia = 0.4 * mass * radius * radius
    unit = cohesion / (stiffness / cohesion)
    for c in range(3):
        accel = unit * sums[c] / mass
        if c == 2:
            accel = accel - 1.0
        out[c, 0] = drifted[c]
        out[3 + c, 0] = drifted[3 + c] + 0.5 * time_step * (drifted[9 + c] + accel)
        out[6 + c, 0] = drifted[6 + c] + time_step * (unit * radius * sums[3 + c]) / inertia
        out[9 + c, 0] = accel
    out[12, 0] = radius


def per_device(spheres, new_home, ghost_list, tile_pairs, tile_count):
    comps, _, blocks, width = spheres.shape
    ghosts = ghost_list.shape[1]
    entries = blocks + 9 * ghosts
    vmem = pl.BlockSpec(memory_space=pltpu.VMEM)
    smem = pl.BlockSpec(memory_space=pltpu.SMEM)
    f32 = jnp.float32
    drifted, pool, counts = pl.pallas_call(
        exchange_kernel,
        out_shape=[
            jax.ShapeDtypeStruct((comps, blocks, width), f32),
            jax.ShapeDtypeStruct((entries, ROWS, width), f32),
            jax.ShapeDtypeStruct((blocks, width), jnp.int32),
        ],
        in_specs=[vmem, smem, smem, vmem, smem],
        out_specs=[vmem, vmem, vmem],
        scratch_shapes=[
            pltpu.VMEM((SPAN + 1, comps, blocks, width), f32),
            pltpu.VMEM((SPAN, comps, blocks, width), f32),
            pltpu.VMEM((blocks, ROWS, width), f32),
            pltpu.VMEM((ghosts, ROWS, width), f32),
            pltpu.SemaphoreType.DMA((SPAN,)),
            pltpu.SemaphoreType.DMA((SPAN,)),
            pltpu.SemaphoreType.DMA((9,)),
            pltpu.SemaphoreType.DMA((9,)),
        ],
        compiler_params=pltpu.CompilerParams(collective_id=0, has_side_effects=True),
        name="exchange",
    )(spheres[:, 0], new_home, ghost_list, tile_pairs[0].T, tile_count)
    return pl.pallas_call(
        functools.partial(contact_kernel, ghosts),
        out_shape=jax.ShapeDtypeStruct((comps, 1, blocks, width), f32),
        in_specs=[smem, vmem, vmem],
        out_specs=vmem,
        scratch_shapes=[
            pltpu.VMEM((FEATURES, width, width), f32),
            pltpu.VMEM((blocks, 6, 8, width), f32),
            pltpu.VMEM((6, blocks, width), f32),
        ],
        name="contact",
    )(counts, drifted, pool)


def solution(mesh):
    in_specs = (
        P(None, "gy", "gx", None),
        P("gy", "gx"),
        P("gy", "gx"),
        P("gy", "gx", None),
        P("gy", "gx"),
    )
    out_specs = P(None, "gy", "gx", None)
    return jax.shard_map(
        per_device, mesh=mesh, in_specs=in_specs, out_specs=out_specs, check_vma=False
    )
```

```python
import functools

import jax
import jax.numpy as jnp
from jax import lax
from jax.experimental import pallas as pl
from jax.experimental.pallas import tpu as pltpu
from jax.sharding import PartitionSpec as P

SPAN = 3
MESH = pl.DeviceIdType.MESH

time_step = 0.01
stiffness = 200.0
damp_normal = 20.0
damp_tangent = 10.0
cohesion = 10.0
density = 240.0

ROWS = 16
FEATURES = 11
TOGETHER = 1


def exchange_kernel(
    spheres, home, lent_list, pairs, count, drifted, pool, counts, sections, arrived, mine, lent, send_sem, recv_sem, gsend_sem, grecv_sem
):
    comps, blocks, width = spheres.shape
    ghosts = lent_list.shape[1]
    nx = lax.axis_size("gx")
    ny = lax.axis_size("gy")
    gx = lax.axis_index("gx")
    gy = lax.axis_index("gy")

    def peer(dx, dy):
        return {"gx": lax.rem(gx + dx + nx, nx), "gy": lax.rem(gy + dy + ny, ny)}

    steps = [(dr, dg) for dr in (-1, 0, 1) for dg in (-1, 0, 1)]
    barrier = pltpu.get_barrier_semaphore()
    for dr, dg in steps:
        if (dr, dg) != (0, 0):
            pl.semaphore_signal(barrier, inc=1, device_id=peer(dg, dr), device_id_type=MESH)
    for off in range(2, SPAN + 1):
        pl.semaphore_signal(barrier, inc=1, device_id=peer(-off, 0), device_id_type=MESH)

    slot = lax.broadcasted_iota(jnp.int32, (blocks, width), 0)
    for off in range(SPAN, -1, -1):
        want = slot + lax.rem(gx + off, nx) * blocks
        masks = [want == home[0, b] for b in range(blocks)]
        for c in range(comps):
            row = jnp.zeros((blocks, width), jnp.float32)
            for b in range(blocks):
                row = jnp.where(masks[b], jnp.broadcast_to(spheres[c, b : b + 1, :], (blocks, width)), row)
            sections[off, c] = row

    pl.semaphore_wait(barrier, 8 + SPAN - 1)
    copies = []
    for off in range(SPAN, 0, -1):
        copy = pltpu.make_async_remote_copy(
            src_ref=sections.at[off],
            dst_ref=arrived.at[off - 1],
            send_sem=send_sem.at[off - 1],
            recv_sem=recv_sem.at[off - 1],
            device_id=peer(off, 0),
            device_id_type=MESH,
        )
        copy.start()
        copies.append(copy)

    cap = pairs.shape[1]
    valid = lax.broadcasted_iota(jnp.int32, (1, cap), 1) < count[0, 0]
    left = jnp.where(valid, pairs[0:1, :], -1)
    right = jnp.where(valid, pairs[1:2, :], -1)
    group = width // 4
    entries = pool.shape[0]
    right = jnp.where(left == right, entries, right)
    hot_left = (lax.broadcasted_iota(jnp.int32, (width, cap), 0) == left).astype(jnp.float32)
    hot_right = (lax.broadcasted_iota(jnp.int32, (group, cap), 0) == right).astype(jnp.float32)
    many = lax.dot_general(hot_right, hot_left, (((1,), (1,)), ((), ())), preferred_element_type=jnp.float32)
    entry = lax.broadcasted_iota(jnp.int32, (group, width), 0)
    lane = lax.broadcasted_iota(jnp.int32, (group, width), 1)
    listed = jnp.logical_and(many > 0, entry < entries)
    ones = jnp.where(listed, 1.0, 0.0)
    before = (
        lax.broadcasted_iota(jnp.int32, (group, group), 1) < lax.broadcasted_iota(jnp.int32, (group, group), 0)
    ).astype(jnp.float32)
    place = jnp.dot(before, ones, preferred_element_type=jnp.float32)
    part = lane // group
    seat = (lane % group).astype(jnp.float32)
    for i in range(blocks):
        spot = jnp.broadcast_to(place[:, i : i + 1], (group, width))
        here = jnp.broadcast_to(ones[:, i : i + 1], (group, width))
        times = jnp.broadcast_to(many[:, i : i + 1], (group, width))
        hit = jnp.where(spot == seat, here, 0.0)
        value = jnp.where(part == 0, hit * entry.astype(jnp.float32), hit * times)
        value = jnp.where(part == 2, here, value)
        value = jnp.where(part == 3, jnp.where(entry == entries, times, 0.0), value)
        counts[i : i + 1, :] = jnp.sum(value, axis=0, keepdims=True).astype(jnp.int32)

    for copy in copies:
        copy.wait()

    def moved(c):
        total = sections[0, c]
        for off in range(SPAN):
            total = total + arrived[off, c]
        return total

    rows = [moved(c) for c in range(comps)]
    for c in range(3):
        rows[c] = rows[c] + time_step * rows[3 + c] + 0.5 * time_step * time_step * rows[9 + c]
    for c in range(comps):
        drifted[c] = rows[c]
    scale = stiffness / cohesion
    radius = rows[12]
    feats = [scale * rows[c] for c in range(3)] + [rows[c] for c in range(3, 6)]
    feats += [radius * rows[c] for c in range(6, 9)] + [scale * radius, 1.0 / (scale * radius)]
    mine[...] = jnp.zeros_like(mine)
    for f in range(FEATURES):
        for b in range(blocks):
            mine[b, f : f + 1, :] = feats[f][b : b + 1, :]
    pool[0:blocks] = mine[...]
    for g in range(ghosts):
        lent[g] = mine[lent_list[0, g]]
        pool[blocks + 4 * ghosts + g] = jnp.zeros((ROWS, width), jnp.float32)
    copies = []
    for k, (dr, dg) in enumerate(steps):
        if (dr, dg) == (0, 0):
            continue
        copy = pltpu.make_async_remote_copy(
            src_ref=lent,
            dst_ref=pool.at[pl.ds(blocks + k * ghosts, ghosts)],
            send_sem=gsend_sem.at[k],
            recv_sem=grecv_sem.at[k],
            device_id=peer(-dg, -dr),
            device_id_type=MESH,
        )
        copy.start()
        copies.append(copy)
    for copy in copies:
        copy.wait()


def pair_sums(left, right, weight, same):
    xa, va, ua, ra, ia = left[0:3], left[3:6], left[6:9], left[9], left[10]
    xb, vb, ub, rb, ib = right[0:3], right[3:6], right[6:9], right[9], right[10]
    sep = [xa[c] - xb[c] for c in range(3)]
    square = sep[0] * sep[0] + sep[1] * sep[1] + sep[2] * sep[2]
    inv = lax.rsqrt(square)
    depth = (ra + rb) - square * inv
    touch = depth > 0
    if same is not None:
        touch = jnp.logical_and(touch, jnp.logical_not(same))
        inv = jnp.where(touch, inv, 0.0)
    rc = jnp.where(touch, depth * lax.rsqrt(depth * (ia + ib)), 0.0) * weight
    depth = jnp.where(touch, depth, 0.0)
    n = [s * inv for s in sep]
    dv = [va[c] - vb[c] for c in range(3)]
    spin = [ua[c] + ub[c] for c in range(3)]
    vn = dv[0] * n[0] + dv[1] * n[1] + dv[2] * n[2]
    slip = [
        rc * (dv[0] - (spin[1] * n[2] - spin[2] * n[1])),
        rc * (dv[1] - (spin[2] * n[0] - spin[0] * n[2])),
        rc * (dv[2] - (spin[0] * n[1] - spin[1] * n[0])),
    ]
    push = rc * (depth - 1.0 - vn)
    return [push * n[c] - slip[c] for c in range(3)] + [
        n[1] * slip[2] - n[2] * slip[1],
        n[2] * slip[0] - n[0] * slip[2],
        n[0] * slip[1] - n[1] * slip[0],
    ]


def contact_kernel(together, plan, drifted, pool, out, spread, acc, sums):
    comps, blocks, width = drifted.shape
    group = width // 4

    def tiles(entries, weights, same):
        right = [[jnp.broadcast_to(pool[j, f : f + 1, :], (8, width)) for f in range(FEATURES)] for j in entries]
        for chunk in range(width // 8):
            rows = pl.ds(chunk * 8, 8)
            left = [spread[f, rows, :] for f in range(FEATURES)]
            own = None
            if same:
                own = lax.broadcasted_iota(jnp.int32, (8, width), 0) + chunk * 8 == lax.broadcasted_iota(jnp.int32, (8, width), 1)
            parts = [pair_sums(left, right[k], weights[k], own) for k in range(len(entries))]
            for c in range(6):
                total = parts[0][c]
                for part in parts[1:]:
                    total = total + part[c]
                acc[c, rows, :] = acc[c, rows, :] + total

    def block_step(i, carry):
        for f in range(FEATURES):
            spread[f] = jnp.transpose(jnp.broadcast_to(pool[i, f : f + 1, :], (width, width)))
        acc[...] = jnp.zeros_like(acc)
        number = plan[i, 2 * group]
        own = plan[i, 3 * group]

        @pl.when(own > 0)
        def _():
            tiles([i], [own.astype(jnp.float32)], True)

        def tile_step(step, inner):
            entries, weights = [], []
            for k in range(together):
                at = step * together + k
                real = jnp.minimum(at, number - 1)
                entries.append(plan[i, real])
                weights.append(jnp.where(at < number, plan[i, group + real], 0).astype(jnp.float32))
            tiles(entries, weights, False)
            return inner

        lax.fori_loop(0, (number + together - 1) // together, tile_step, carry)
        for c in range(6):
            sums[c, pl.ds(i, 1), :] = jnp.sum(jnp.transpose(acc[c]), axis=0, keepdims=True)
        return carry

    lax.fori_loop(0, blocks, block_step, 0)

    radius = drifted[12]
    mass = density * (4.0 / 3.0) * jnp.pi * radius * radius * radius
    inertia = 0.4 * mass * radius * radius
    unit = cohesion / (stiffness / cohesion)
    for c in range(3):
        accel = unit * sums[c] / mass
        if c == 2:
            accel = accel - 1.0
        out[c, 0] = drifted[c]
        out[3 + c, 0] = drifted[3 + c] + 0.5 * time_step * (drifted[9 + c] + accel)
        out[6 + c, 0] = drifted[6 + c] + time_step * (unit * radius * sums[3 + c]) / inertia
        out[9 + c, 0] = accel
    out[12, 0] = radius


def per_device(spheres, new_home, ghost_list, tile_pairs, tile_count):
    comps, _, blocks, width = spheres.shape
    ghosts = ghost_list.shape[1]
    entries = blocks + 9 * ghosts
    vmem = pl.BlockSpec(memory_space=pltpu.VMEM)
    smem = pl.BlockSpec(memory_space=pltpu.SMEM)
    f32 = jnp.float32
    drifted, pool, counts = pl.pallas_call(
        exchange_kernel,
        out_shape=[
            jax.ShapeDtypeStruct((comps, blocks, width), f32),
            jax.ShapeDtypeStruct((entries, ROWS, width), f32),
            jax.ShapeDtypeStruct((blocks, width), jnp.int32),
        ],
        in_specs=[vmem, smem, smem, vmem, smem],
        out_specs=[vmem, vmem, vmem],
        scratch_shapes=[
            pltpu.VMEM((SPAN + 1, comps, blocks, width), f32),
            pltpu.VMEM((SPAN, comps, blocks, width), f32),
            pltpu.VMEM((blocks, ROWS, width), f32),
            pltpu.VMEM((ghosts, ROWS, width), f32),
            pltpu.SemaphoreType.DMA((SPAN,)),
            pltpu.SemaphoreType.DMA((SPAN,)),
            pltpu.SemaphoreType.DMA((9,)),
            pltpu.SemaphoreType.DMA((9,)),
        ],
        compiler_params=pltpu.CompilerParams(collective_id=0, has_side_effects=True),
        name="exchange",
    )(spheres[:, 0], new_home, ghost_list, tile_pairs[0].T, tile_count)
    return pl.pallas_call(
        functools.partial(contact_kernel, TOGETHER),
        out_shape=jax.ShapeDtypeStruct((comps, 1, blocks, width), f32),
        in_specs=[smem, vmem, vmem],
        out_specs=vmem,
        scratch_shapes=[
            pltpu.VMEM((FEATURES, width, width), f32),
            pltpu.VMEM((6, width, width), f32),
            pltpu.VMEM((6, blocks, width), f32),
        ],
        name="contact",
    )(counts, drifted, pool)


def solution(mesh):
    in_specs = (
        P(None, "gy", "gx", None),
        P("gy", "gx"),
        P("gy", "gx"),
        P("gy", "gx", None),
        P("gy", "gx"),
    )
    out_specs = P(None, "gy", "gx", None)
    return jax.shard_map(
        per_device, mesh=mesh, in_specs=in_specs, out_specs=out_specs, check_vma=False
    )
```

```python
import jax
import jax.numpy as jnp
from jax import lax
from jax.experimental import pallas as pl
from jax.experimental.pallas import tpu as pltpu
from jax.sharding import PartitionSpec as P

SPAN = 3
MESH = pl.DeviceIdType.MESH

time_step = 0.01
stiffness = 200.0
damp_normal = 20.0
damp_tangent = 10.0
cohesion = 10.0
density = 240.0

ROWS = 16
FEATURES = 11
ORDER = (0, 1, 2, 3, 4, 5, 6, 7, 8, 12, 9, 10, 11)
EARLY = 10


def exchange_kernel(
    spheres, home, lent_list, pairs, count, drifted, pool, counts, sections, arrived, ahead, mine, lent, send_sem, recv_sem, gsend_sem, grecv_sem
):
    comps, blocks, width = spheres.shape
    ghosts = lent_list.shape[1]
    nx = lax.axis_size("gx")
    ny = lax.axis_size("gy")
    gx = lax.axis_index("gx")
    gy = lax.axis_index("gy")

    def peer(dx, dy):
        return {"gx": lax.rem(gx + dx + nx, nx), "gy": lax.rem(gy + dy + ny, ny)}

    steps = [(dr, dg) for dr in (-1, 0, 1) for dg in (-1, 0, 1)]
    barrier = pltpu.get_barrier_semaphore()
    for dr, dg in steps:
        if (dr, dg) != (0, 0):
            pl.semaphore_signal(barrier, inc=1, device_id=peer(dg, dr), device_id_type=MESH)
    for off in range(2, SPAN + 1):
        pl.semaphore_signal(barrier, inc=1, device_id=peer(-off, 0), device_id_type=MESH)

    for c in range(comps):
        row = spheres[c]
        if c < 3:
            row = row + time_step * spheres[3 + c] + 0.5 * time_step * time_step * spheres[9 + c]
        ahead[ORDER.index(c)] = row

    slot = lax.broadcasted_iota(jnp.int32, (blocks, width), 0)
    for off in range(SPAN, -1, -1):
        want = slot + lax.rem(gx + off, nx) * blocks
        masks = [want == home[0, b] for b in range(blocks)]
        for c in range(comps):
            row = jnp.zeros((blocks, width), jnp.float32)
            for b in range(blocks):
                row = jnp.where(masks[b], jnp.broadcast_to(ahead[c, b : b + 1, :], (blocks, width)), row)
            sections[off, c] = row

    pl.semaphore_wait(barrier, 8 + SPAN - 1)
    copies = []
    for late, part in enumerate((pl.ds(0, EARLY), pl.ds(EARLY, comps - EARLY))):
        for off in range(SPAN, 0, -1):
            copy = pltpu.make_async_remote_copy(
                src_ref=sections.at[off, part],
                dst_ref=arrived.at[off - 1, part],
                send_sem=send_sem.at[late, off - 1],
                recv_sem=recv_sem.at[late, off - 1],
                device_id=peer(off, 0),
                device_id_type=MESH,
            )
            copy.start()
            copies.append(copy)
    late_copies = copies[SPAN:]
    copies = copies[:SPAN]

    cap = pairs.shape[1]
    valid = lax.broadcasted_iota(jnp.int32, (1, cap), 1) < count[0, 0]
    left = jnp.where(valid, pairs[0:1, :], -1)
    right = jnp.where(valid, pairs[1:2, :], -1)
    group = width // 4
    entries = pool.shape[0]
    right = jnp.where(left == right, entries, right)
    hot_left = (lax.broadcasted_iota(jnp.int32, (width, cap), 0) == left).astype(jnp.float32)
    hot_right = (lax.broadcasted_iota(jnp.int32, (group, cap), 0) == right).astype(jnp.float32)
    many = lax.dot_general(hot_right, hot_left, (((1,), (1,)), ((), ())), preferred_element_type=jnp.float32)
    hot_left = (lax.broadcasted_iota(jnp.int32, (group, cap), 0) == left).astype(jnp.float32)
    hot_right = (lax.broadcasted_iota(jnp.int32, (width, cap), 0) == right).astype(jnp.float32)
    back = lax.dot_general(hot_left, hot_right, (((1,), (1,)), ((), ())), preferred_element_type=jnp.float32)
    entry = lax.broadcasted_iota(jnp.int32, (group, width), 0)
    lane = lax.broadcasted_iota(jnp.int32, (group, width), 1)
    listed = jnp.logical_and(many > 0, entry < entries)
    mutual = jnp.logical_and(jnp.logical_and(listed, back > 0), jnp.logical_and(entry < blocks, lane < blocks))
    both = jnp.where(jnp.logical_and(mutual, entry > lane), 1.0, 0.0)
    ones = jnp.where(jnp.logical_and(listed, jnp.logical_not(mutual)), 1.0, 0.0)
    before = (
        lax.broadcasted_iota(jnp.int32, (group, group), 1) < lax.broadcasted_iota(jnp.int32, (group, group), 0)
    ).astype(jnp.float32)
    place = jnp.dot(before, ones, preferred_element_type=jnp.float32)
    place = jnp.where(both > 0, group - 1.0 - jnp.dot(before, both, preferred_element_type=jnp.float32), place)
    part = lane // group
    seat = (lane % group).astype(jnp.float32)
    for i in range(blocks):
        shape = (group, width)
        spot = jnp.broadcast_to(place[:, i : i + 1], shape)
        one = jnp.broadcast_to(ones[:, i : i + 1], shape)
        two = jnp.broadcast_to(both[:, i : i + 1], shape)
        times = jnp.broadcast_to(many[:, i : i + 1], shape)
        hit = jnp.where(spot == seat, one + two, 0.0)
        value = jnp.where(part == 0, hit * entry.astype(jnp.float32), hit * times)
        value = jnp.where(part == 3, hit * jnp.broadcast_to(back[:, i : i + 1], shape), value)
        tally = jnp.where(seat == 0.0, one, jnp.where(seat == 1.0, two, jnp.where(entry == entries, times, 0.0)))
        value = jnp.where(part == 2, tally, value)
        counts[i : i + 1, :] = jnp.sum(value, axis=0, keepdims=True).astype(jnp.int32)

    for copy in copies:
        copy.wait()

    def moved(c):
        total = sections[0, c]
        for off in range(SPAN):
            total = total + arrived[off, c]
        return total

    rows = {ORDER[k]: moved(k) for k in range(EARLY)}
    for c in rows:
        drifted[c] = rows[c]
    scale = stiffness / cohesion
    radius = rows[12]
    feats = [scale * rows[c] for c in range(3)] + [rows[c] for c in range(3, 6)]
    feats += [radius * rows[c] for c in range(6, 9)] + [scale * radius, 1.0 / (scale * radius)]
    mine[...] = jnp.zeros_like(mine)
    for f in range(FEATURES):
        for b in range(blocks):
            mine[b, f : f + 1, :] = feats[f][b : b + 1, :]
    pool[0:blocks] = mine[...]
    for g in range(ghosts):
        lent[g] = mine[lent_list[0, g]]
        pool[blocks + 4 * ghosts + g] = jnp.zeros((ROWS, width), jnp.float32)
    copies = []
    for k, (dr, dg) in enumerate(steps):
        if (dr, dg) == (0, 0):
            continue
        copy = pltpu.make_async_remote_copy(
            src_ref=lent,
            dst_ref=pool.at[pl.ds(blocks + k * ghosts, ghosts)],
            send_sem=gsend_sem.at[k],
            recv_sem=grecv_sem.at[k],
            device_id=peer(-dg, -dr),
            device_id_type=MESH,
        )
        copy.start()
        copies.append(copy)
    for copy in late_copies:
        copy.wait()
    for k in range(EARLY, comps):
        drifted[ORDER[k]] = moved(k)
    for copy in copies:
        copy.wait()


def pair_sums(left, right, weight, same):
    xa, va, ua, ra, ia = left[0:3], left[3:6], left[6:9], left[9], left[10]
    xb, vb, ub, rb, ib = right[0:3], right[3:6], right[6:9], right[9], right[10]
    sep = [xa[c] - xb[c] for c in range(3)]
    square = sep[0] * sep[0] + sep[1] * sep[1] + sep[2] * sep[2]
    inv = lax.rsqrt(square)
    depth = (ra + rb) - square * inv
    touch = depth > 0
    if same is not None:
        touch = jnp.logical_and(touch, jnp.logical_not(same))
        inv = jnp.where(touch, inv, 0.0)
    rc = jnp.where(touch, depth * lax.rsqrt(depth * (ia + ib)), 0.0) * weight
    depth = jnp.where(touch, depth, 0.0)
    n = [s * inv for s in sep]
    dv = [va[c] - vb[c] for c in range(3)]
    spin = [ua[c] + ub[c] for c in range(3)]
    vn = dv[0] * n[0] + dv[1] * n[1] + dv[2] * n[2]
    slip = [
        rc * (dv[0] - (spin[1] * n[2] - spin[2] * n[1])),
        rc * (dv[1] - (spin[2] * n[0] - spin[0] * n[2])),
        rc * (dv[2] - (spin[0] * n[1] - spin[1] * n[0])),
    ]
    push = rc * (depth - 1.0 - vn)
    return [push * n[c] - slip[c] for c in range(3)] + [
        n[1] * slip[2] - n[2] * slip[1],
        n[2] * slip[0] - n[0] * slip[2],
        n[0] * slip[1] - n[1] * slip[0],
    ]


def contact_kernel(plan, drifted, pool, out, spread, acc, mirror, sums):
    comps, blocks, width = drifted.shape
    group = width // 4

    mirror[...] = jnp.zeros_like(mirror)

    def tile(j, weight, same=False, ratio=None):
        right = [jnp.broadcast_to(pool[j, f : f + 1, :], (8, width)) for f in range(FEATURES)]
        total = [jnp.zeros((8, width), jnp.float32)] * 6
        for chunk in range(width // 8):
            rows = pl.ds(chunk * 8, 8)
            left = [spread[f, rows, :] for f in range(FEATURES)]
            own = None
            if same:
                own = lax.broadcasted_iota(jnp.int32, (8, width), 0) + chunk * 8 == lax.broadcasted_iota(jnp.int32, (8, width), 1)
            part = pair_sums(left, right, weight, own)
            for c in range(6):
                acc[c, rows, :] = acc[c, rows, :] + part[c]
            if ratio is not None:
                total = [total[c] + part[c] for c in range(6)]
        if ratio is not None:
            for c in range(6):
                mirror[j, c] = mirror[j, c] + ratio * total[c]

    def block_step(i, carry):
        for f in range(FEATURES):
            spread[f] = jnp.transpose(jnp.broadcast_to(pool[i, f : f + 1, :], (width, width)))
        acc[...] = jnp.zeros_like(acc)
        alone = plan[i, 2 * group]
        paired = plan[i, 2 * group + 1]
        own = plan[i, 2 * group + 2]

        @pl.when(own > 0)
        def _():
            tile(i, own.astype(jnp.float32), same=True)

        def alone_step(at, inner):
            tile(plan[i, at], plan[i, group + at].astype(jnp.float32))
            return inner

        def paired_step(step, inner):
            at = group - 1 - step
            weight = jnp.full((8, width), plan[i, group + at].astype(jnp.float32))
            back = jnp.full((8, width), plan[i, 3 * group + at].astype(jnp.float32))
            tile(plan[i, at], weight, ratio=back / weight)
            return inner

        lax.fori_loop(0, alone, alone_step, carry)
        lax.fori_loop(0, paired, paired_step, carry)
        for c in range(6):
            sums[c, pl.ds(i, 1), :] = jnp.sum(jnp.transpose(acc[c]), axis=0, keepdims=True)
        return carry

    lax.fori_loop(0, blocks, block_step, 0)
    for i in range(blocks):
        for c in range(6):
            row = jnp.sum(mirror[i, c], axis=0, keepdims=True)
            row = -row if c < 3 else row
            sums[c, i : i + 1, :] = sums[c, i : i + 1, :] + row

    radius = drifted[12]
    mass = density * (4.0 / 3.0) * jnp.pi * radius * radius * radius
    inertia = 0.4 * mass * radius * radius
    unit = cohesion / (stiffness / cohesion)
    for c in range(3):
        accel = unit * sums[c] / mass
        if c == 2:
            accel = accel - 1.0
        out[c, 0] = drifted[c]
        out[3 + c, 0] = drifted[3 + c] + 0.5 * time_step * (drifted[9 + c] + accel)
        out[6 + c, 0] = drifted[6 + c] + time_step * (unit * radius * sums[3 + c]) / inertia
        out[9 + c, 0] = accel
    out[12, 0] = radius


def per_device(spheres, new_home, ghost_list, tile_pairs, tile_count):
    comps, _, blocks, width = spheres.shape
    ghosts = ghost_list.shape[1]
    entries = blocks + 9 * ghosts
    vmem = pl.BlockSpec(memory_space=pltpu.VMEM)
    smem = pl.BlockSpec(memory_space=pltpu.SMEM)
    f32 = jnp.float32
    drifted, pool, counts = pl.pallas_call(
        exchange_kernel,
        out_shape=[
            jax.ShapeDtypeStruct((comps, blocks, width), f32),
            jax.ShapeDtypeStruct((entries, ROWS, width), f32),
            jax.ShapeDtypeStruct((blocks, width), jnp.int32),
        ],
        in_specs=[vmem, smem, smem, vmem, smem],
        out_specs=[vmem, vmem, vmem],
        scratch_shapes=[
            pltpu.VMEM((SPAN + 1, comps, blocks, width), f32),
            pltpu.VMEM((SPAN, comps, blocks, width), f32),
            pltpu.VMEM((comps, blocks, width), f32),
            pltpu.VMEM((blocks, ROWS, width), f32),
            pltpu.VMEM((ghosts, ROWS, width), f32),
            pltpu.SemaphoreType.DMA((2, SPAN)),
            pltpu.SemaphoreType.DMA((2, SPAN)),
            pltpu.SemaphoreType.DMA((9,)),
            pltpu.SemaphoreType.DMA((9,)),
        ],
        compiler_params=pltpu.CompilerParams(collective_id=0, has_side_effects=True),
        name="exchange",
    )(spheres[:, 0], new_home, ghost_list, tile_pairs[0].T, tile_count)
    return pl.pallas_call(
        contact_kernel,
        out_shape=jax.ShapeDtypeStruct((comps, 1, blocks, width), f32),
        in_specs=[smem, vmem, vmem],
        out_specs=vmem,
        scratch_shapes=[
            pltpu.VMEM((FEATURES, width, width), f32),
            pltpu.VMEM((6, width, width), f32),
            pltpu.VMEM((blocks, 6, 8, width), f32),
            pltpu.VMEM((6, blocks, width), f32),
        ],
        name="contact",
    )(counts, drifted, pool)


def solution(mesh):
    in_specs = (
        P(None, "gy", "gx", None),
        P("gy", "gx"),
        P("gy", "gx"),
        P("gy", "gx", None),
        P("gy", "gx"),
    )
    out_specs = P(None, "gy", "gx", None)
    return jax.shard_map(
        per_device, mesh=mesh, in_specs=in_specs, out_specs=out_specs, check_vma=False
    )
```
